32 devices in a mesh: groups: 2 (over x), chan: 16 (over z, y, core).
Axes of the slice: x: 2, y: 2, z: 4, core: 2. Of those that a mesh axis runs over, the one named last changes fastest.
Arguments:
- records: bfloat16 [256, 32, 2048], P(('groups', 'chan')), parts along dimension 0, may hold values from -6 to 6
- window_valid: float32 [256, 32], P(('groups', 'chan')), parts along dimension 0, may hold values from 0 to 1, as said below
- band_low: int32 [256], P(('groups', 'chan')), parts along dimension 0, may hold values from 0 to 255
- band_high: int32 [256], P(('groups', 'chan')), parts along dimension 0, may hold values from 768 to 1024
- pair_counts: int32 [32], P('groups'), parts along dimension 0, may hold values from 1 to 4, 32 in all
- partners: int32 [32, 4], P('groups'), parts along dimension 0, may hold values from 0 to 15
Outputs:
- stacks: bfloat16 [32, 4, 1024, 128], P(('groups', 'chan')), parts along dimension 0
The draws below stay inside these ranges and needn't reach their ends.
There are 2 independent parts, one for each index of `groups`. The reference program is written for one: setup_inputs(seed, part) draws one part's arguments, and reference() takes and returns one part's arrays. A program takes and returns all parts, laid end to end along the dimension named above; each array names one. Nothing has to cross between parts.
Inputs may be any that keep to these rules, and one draw needn't show every extreme that they name: `window_valid`: 0 marks a window without data; some channels have no window with data. `pair_counts`: the counts sum to 32, and the largest is 4.
All inputs are finite; a program needn't handle non-finite values.
Results may differ from the reference program's by a relative error of at most 0.0065.
Values may be sent and summed in bfloat16 or wider, within the bound.
A program may use at most 128 MiB of HBM per device.

```python
import math
import jax
import jax.numpy as jnp
import numpy as np
from jax import lax

F = 1024
L = 2048
CH_DEV = 8
W = 32
P_MAX = 4
SMOOTH = 8
C = 128
N_CHAN = 16


def draw_window_valid(key, part):
    dead_key, window_key, level_key = jax.random.split(jax.random.fold_in(key, 11), 3)
    alive = jax.random.randint(dead_key, (C, 1), 0, 8) > 0
    holding = jax.random.randint(window_key, (C, W), 0, 4) > 0
    level = jnp.exp(jax.random.uniform(level_key, (C, W), jnp.float32, math.log(0.1), 0.0))
    return jnp.where(alive & holding, level, 0.0).astype(jnp.float32)


def with_ends(entries, own_key, low, largest):
    longest = entries.shape.index(max(entries.shape))
    spots = []
    for shift in (0, 1):
        where = [jax.random.randint(jax.random.fold_in(own_key, axis), (), 0, length) for axis, length in enumerate(entries.shape)]
        where[longest] = (where[longest] + shift) % entries.shape[longest]
        spots.append(tuple(where))
    return entries.at[spots[0]].set(low).at[spots[1]].set(largest)


def levels(own_key, shape, shards, smallest, top_value):
    def one(dim, parts):
        heights = jax.random.uniform(jax.random.fold_in(jax.random.fold_in(own_key, 6), dim), (parts,), jnp.float32, smallest / len(shards), top_value / len(shards))
        return jnp.repeat(jnp.exp(heights), shape[dim] // parts).reshape((-1,) + (1,) * (len(shape) - dim - 1))

    gain = one(*shards[0])
    for cut in shards[1:]:
        gain = gain * one(*cut)
    return gain


def length_profile(amount, total, most, slope):
    portions = [(1 << 20) // math.isqrt(grade ** slope) + 1 for grade in range(2, amount + 1)]
    rest, given = total - most - (amount - 1), [1] * (amount - 1)
    while rest > 0:
        movable = [i for i in range(amount - 1) if given[i] < most]
        whole, budget = sum([portions[i] for i in movable]), rest
        for i in movable:
            extra = min(most - given[i], max(1, budget * portions[i] // whole), rest)
            given[i] = given[i] + extra
            rest = rest - extra
    return np.array([most] + given)


def uneven(key, count, total, limit, slope):
    if count == 2:
        one = jax.random.randint(key, (), max(1, total - limit), min(limit, total - 1) + 1)
        return jnp.stack([one, total - one])
    lengths = jnp.asarray(length_profile(count, total, limit, slope), jnp.int32)
    couples = (count - 1) // 2
    giver, taker = lengths[1:1 + 2 * couples:2], lengths[2:2 + 2 * couples:2]
    margin = jnp.minimum(giver - 1, limit - taker)
    shifted = jax.random.randint(jax.random.fold_in(key, 1), (couples,), 0, 1 << 20) % (margin + 1)
    lengths = lengths.at[1:1 + 2 * couples:2].set(giver - shifted).at[2:2 + 2 * couples:2].set(taker + shifted)
    return lengths[jax.random.permutation(jax.random.fold_in(key, 2), count)]


def noise(rng, dims, spread, reach, pieces=(), kind=jnp.bfloat16):
    array = jax.random.normal(rng, dims, jnp.float32) * spread
    if len(pieces) > 0:
        array = levels(rng, dims, pieces, -0.22, 0.18) * array
    return jnp.clip(array, min=-reach, max=reach).astype(kind)


def setup_inputs(seed: int = 0, part: int = 0) -> dict:
    arg_keys = jax.random.split(jax.random.key(seed), 7)
    part_keys = jax.random.split(jax.random.fold_in(arg_keys[6], part), 7)
    return {
        "records": noise(part_keys[0], (C, W, L), 1.0, 6.0, ((0, 16),)),
        "window_valid": draw_window_valid(jax.random.fold_in(jax.random.fold_in(arg_keys[6], part), 71), part),
        "band_low": with_ends(jax.random.randint(part_keys[2], (C,), 0, F // 4), jax.random.fold_in(part_keys[2], 1), 0, (F // 4) - 1).astype(jnp.int32),
        "band_high": with_ends(jax.random.randint(part_keys[3], (C,), 3 * F // 4, F + 1), jax.random.fold_in(part_keys[3], 1), 3 * F // 4, F).astype(jnp.int32),
        "pair_counts": uneven(part_keys[4], N_CHAN, 2 * N_CHAN, P_MAX, 2).astype(jnp.int32),
        "partners": with_ends(jax.random.randint(part_keys[5], (N_CHAN, P_MAX), 0, N_CHAN), jax.random.fold_in(part_keys[5], 1), 0, N_CHAN - 1).astype(jnp.int32),
    }


def dft_table(length, first_bin, bin_count):
    sample_index = lax.broadcasted_iota(jnp.int32, (length, bin_count), 0)
    bin_index = lax.broadcasted_iota(jnp.int32, (length, bin_count), 1) + first_bin
    phase_step = sample_index * bin_index % length
    angles = phase_step.astype(jnp.float32) * (2.0 * math.pi / length)
    return jnp.concatenate([jnp.cos(angles), -jnp.sin(angles)], axis=1).astype(jnp.bfloat16)

def finish(spectrum, band_low, band_high, channels, windows):
    bin_total = spectrum.shape[1]
    magnitude = jnp.sqrt(spectrum[0] * spectrum[0] + spectrum[1] * spectrum[1])
    offsets = lax.broadcasted_iota(jnp.int32, (bin_total, bin_total), 0) - lax.broadcasted_iota(jnp.int32, (bin_total, bin_total), 1)
    window = (jnp.abs(offsets) <= SMOOTH).astype(jnp.float32)
    smoothed = jnp.dot(window, magnitude, precision=lax.Precision.HIGHEST) / lax.optimization_barrier(jnp.sum(window, axis=1, keepdims=True))
    divisor = jnp.maximum(smoothed, 1.0).reshape(bin_total, channels, windows)
    bin_index = lax.broadcasted_iota(jnp.int32, (bin_total, channels, 1), 0)
    inside = ((bin_index >= band_low[None, :, None]) & (bin_index < band_high[None, :, None])).astype(jnp.float32)
    shaped = spectrum.reshape(2, bin_total, channels, windows)
    return (shaped / divisor * inside).astype(jnp.bfloat16).reshape(2, bin_total, channels * windows)

def reference(records, window_valid, band_low, band_high, pair_counts, partners):
    readers = N_CHAN
    length = 2 * F
    dft_full = dft_table(length, 0, F)
    record_blocks = records.reshape(readers, CH_DEV, W, length)
    valid_blocks = window_valid.reshape(readers, CH_DEV, W)
    low_blocks = band_low.reshape(readers, CH_DEV)
    high_blocks = band_high.reshape(readers, CH_DEV)

    def prepare(inputs):
        block_records, block_valid, block_low, block_high = inputs
        one_bit = (jnp.sign(block_records.astype(jnp.float32)) * block_valid.astype(jnp.float32)[:, :, None]).astype(jnp.bfloat16)
        one_bit = one_bit.reshape(CH_DEV * W, length)
        spectrum = lax.dot_general(dft_full, one_bit, (((0,), (1,)), ((), ())), preferred_element_type=jnp.float32)
        spectrum = spectrum.reshape(2, F, CH_DEV * W)
        return finish(spectrum, block_low, block_high, CH_DEV, W)
    whitened = lax.map(prepare, (record_blocks, valid_blocks, low_blocks, high_blocks))
    spectra = whitened.reshape(readers, 2, F, CH_DEV, W)
    valid_all = window_valid.astype(jnp.float32).reshape(readers, CH_DEV, W)

    def one_reader(reader):
        own = spectra[reader].astype(jnp.float32)
        partner_ids = partners[reader]
        others = jnp.take(spectra, partner_ids, axis=0).astype(jnp.float32)
        real_part = jnp.einsum('fim,pfjm->pfij', own[0], others[:, 0]) + jnp.einsum('fim,pfjm->pfij', own[1], others[:, 1])
        imag_part = jnp.einsum('fim,pfjm->pfij', own[1], others[:, 0]) - jnp.einsum('fim,pfjm->pfij', own[0], others[:, 1])
        common = jnp.einsum('im,pjm->pij', valid_all[reader], jnp.take(valid_all, partner_ids, axis=0), precision=lax.Precision.HIGHEST)
        in_use = (jnp.arange(P_MAX, dtype=jnp.int32) < pair_counts[reader]).astype(jnp.float32)
        weight = in_use[:, None, None] / jnp.maximum(common, 1.0)
        both = jnp.stack([real_part, imag_part], axis=2) * weight[:, None, None]
        return both.reshape(P_MAX, F, 2 * CH_DEV * CH_DEV).astype(jnp.bfloat16)
    return lax.map(one_reader, jnp.arange(readers, dtype=jnp.int32))
```

```python
import functools
import math

import jax
import jax.numpy as jnp
import ml_dtypes
import numpy as np
from jax import lax
from jax.experimental import pallas as pl
from jax.experimental.pallas import tpu as pltpu
from jax.sharding import PartitionSpec as P

SMOOTH = 8


def dft_table(length, first_bin, bin_count):
    sample_index = lax.broadcasted_iota(jnp.int32, (length, bin_count), 0)
    bin_index = lax.broadcasted_iota(jnp.int32, (length, bin_count), 1) + first_bin
    phase_step = sample_index * bin_index % length
    angles = phase_step.astype(jnp.float32) * (2.0 * math.pi / length)
    return jnp.concatenate([jnp.cos(angles), -jnp.sin(angles)], axis=1).astype(jnp.bfloat16)


def finish(spectrum, band_low, band_high, channels, windows):
    bin_total = spectrum.shape[1]
    magnitude = jnp.sqrt(spectrum[0] * spectrum[0] + spectrum[1] * spectrum[1])
    padded = jnp.pad(magnitude, ((SMOOTH, SMOOTH), (0, 0)))
    summed = padded[0:bin_total]
    for offset in range(1, 2 * SMOOTH + 1):
        summed = summed + padded[offset : offset + bin_total]
    bin_column = lax.broadcasted_iota(jnp.int32, (bin_total, 1), 0)
    in_range = (
        jnp.minimum(bin_column + SMOOTH, bin_total - 1) - jnp.maximum(bin_column - SMOOTH, 0) + 1
    )
    smoothed = summed / in_range.astype(jnp.float32)
    divisor = jnp.maximum(smoothed, 1.0).reshape(bin_total, channels, windows)
    bin_index = lax.broadcasted_iota(jnp.int32, (bin_total, channels, 1), 0)
    inside = (
        (bin_index >= band_low[None, :, None]) & (bin_index < band_high[None, :, None])
    ).astype(jnp.float32)
    shaped = spectrum.reshape(2, bin_total, channels, windows)
    return (
        (shaped / divisor * inside).astype(jnp.bfloat16).reshape(2, bin_total, channels * windows)
    )


def whiten(records, window_valid, band_low, band_high):
    channels, windows, length = records.shape
    bin_total = length // 2
    row_total = channels * windows
    one_bit = (jnp.sign(records.astype(jnp.float32)) * window_valid[:, :, None]).astype(
        jnp.bfloat16
    )
    one_bit = one_bit.reshape(row_total, length)
    blocks = []
    for first_bin in range(0, bin_total, 256):
        dft_block = dft_table(length, first_bin, 256)
        partial_spec = lax.dot_general(
            dft_block, one_bit, (((0,), (1,)), ((), ())), preferred_element_type=jnp.float32
        )
        blocks.append(partial_spec.reshape(2, 256, row_total))
    spectrum = jnp.concatenate(blocks, axis=1)
    return finish(spectrum, band_low, band_high, channels, windows)


def cross_stack(first_spec, second_spec, first_flags, second_flags, in_use):
    real_part = jnp.einsum(
        "fsim,fsjm->sfij", first_spec[0], second_spec[0], preferred_element_type=jnp.float32
    )
    real_part = real_part + jnp.einsum(
        "fsim,fsjm->sfij", first_spec[1], second_spec[1], preferred_element_type=jnp.float32
    )
    imag_part = jnp.einsum(
        "fsim,fsjm->sfij", first_spec[1], second_spec[0], preferred_element_type=jnp.float32
    )
    imag_part = imag_part - jnp.einsum(
        "fsim,fsjm->sfij", first_spec[0], second_spec[1], preferred_element_type=jnp.float32
    )
    common = jnp.einsum("sim,sjm->sij", first_flags, second_flags, precision=lax.Precision.HIGHEST)
    weight = in_use[:, None, None] / jnp.maximum(common, 1.0)
    both = jnp.stack([real_part, imag_part], axis=2) * weight[:, None, None]
    return both.reshape(both.shape[0], both.shape[1], -1).astype(jnp.bfloat16)


def body(records, window_valid, band_low, band_high, pair_counts, partners):
    channels, windows, length = records.shape
    bin_total = length // 2
    readers, slot_count = partners.shape
    bin_share = bin_total // readers
    whitened = whiten(records, window_valid, band_low, band_high)
    arrived = lax.all_to_all(whitened, "chan", split_axis=1, concat_axis=2, tiled=True)
    spectra = arrived.reshape(2, bin_share, readers, channels, windows)
    copies = jnp.broadcast_to(window_valid[None], (readers, channels, windows))
    valid_all = lax.all_to_all(copies, "chan", split_axis=0, concat_axis=0, tiled=True)
    results = []
    for slot_index in range(slot_count):
        partner_ids = partners[:, slot_index]
        picks = partner_ids[:, None] == jnp.arange(readers, dtype=jnp.int32)[None, :]
        partner_spec = jnp.einsum("rq,cfqim->cfrim", picks.astype(jnp.bfloat16), spectra)
        partner_flags = jnp.einsum(
            "rq,qim->rim", picks.astype(jnp.float32), valid_all, precision=lax.Precision.HIGHEST
        )
        in_use = (slot_index < pair_counts).astype(jnp.float32)
        results.append(cross_stack(spectra, partner_spec, valid_all, partner_flags, in_use))
    stacked = jnp.stack(results, axis=1)
    return lax.all_to_all(stacked, "chan", split_axis=0, concat_axis=2, tiled=True)


LANES = 128


def packed_table(length, share, readers):
    bins = np.arange(readers * share).reshape(readers // 2, 2, share)
    samples = np.arange(length)
    phase = (samples[None, :, None, None] * bins[:, None]) % length
    angles = phase.astype(np.float32) * np.float32(2.0 * math.pi / length)
    table = np.stack([np.cos(angles), -np.sin(angles)], axis=3)
    return table.reshape(readers // 2, length, 4 * share).astype(ml_dtypes.bfloat16)


def packed_band(share):
    lane = np.arange(2 * share) % share
    rows = np.arange(3)[:, None] * share - share + lane[None, :]
    near = np.abs(rows[:, :, None] - lane[None, None, :]) <= SMOOTH
    return (near * 0.5).astype(ml_dtypes.bfloat16)


def fused_kernel(
    n,
    bin_total,
    records,
    valid,
    low,
    high,
    counts,
    partners,
    table,
    band,
    out,
    tables,
    raw,
    signs,
    spec,
    mags,
    send,
    recv,
    valids,
    full,
    turned,
    stacked,
    table_sem,
    valid_send,
    valid_recv,
    spec_send,
    spec_recv,
    out_send,
    out_recv,
    own_sem,
):
    me = lax.axis_index("chan")
    channels, windows, length = records.shape
    share = bin_total // n
    rows = channels * windows
    slots = partners.shape[1]

    def peer(step):
        return lax.rem(me + step, n)

    barrier = pltpu.get_barrier_semaphore()
    for step in range(1, n):
        pl.semaphore_signal(
            barrier, inc=1, device_id={"chan": peer(step)}, device_id_type=pl.DeviceIdType.MESH
        )

    def table_copy(chunk):
        return pltpu.make_async_copy(table.at[chunk], tables.at[chunk], table_sem.at[chunk])

    for chunk in range(n // 2):
        table_copy(chunk).start()

    valids[me] = valid[...]

    def to_signs(part, _):
        at = pl.multiple_of(part * LANES, LANES)
        raw[...] = records[:, :, pl.ds(at, LANES)].astype(jnp.float32).reshape(rows, LANES)
        for pair in range(windows // 2):
            halves = []
            for window in (2 * pair, 2 * pair + 1):
                x = raw[pl.ds(window, channels, stride=windows), :]
                v = valid[:, window : window + 1]
                halves.append(jnp.where(x > 0, v, jnp.where(x < 0, -v, 0.0)))
            signs[pl.ds(pair * 2 * channels, 2 * channels), pl.ds(at, LANES)] = jnp.concatenate(
                halves, axis=0
            ).astype(jnp.bfloat16)
        return 0

    lax.fori_loop(0, length // LANES, to_signs, 0)

    mags[0] = jnp.zeros((rows, LANES), jnp.bfloat16)
    mags[n + 1] = jnp.zeros((rows, LANES), jnp.bfloat16)

    def transform(chunk, _):
        table_copy(chunk).wait()
        x = jnp.dot(signs[...], tables[chunk], preferred_element_type=jnp.float32)
        for half in range(2):
            y = x[:, half * LANES : (half + 1) * LANES]
            spec[2 * chunk + half] = y
            power = y * y
            mags[2 * chunk + half + 1] = jnp.sqrt(power + pltpu.roll(power, share, 1)).astype(
                jnp.bfloat16
            )
        return 0

    lax.fori_loop(0, n // 2, transform, 0)

    pl.semaphore_wait(barrier, n - 1)

    def valid_copy(source, target):
        return pltpu.make_async_remote_copy(
            src_ref=valids.at[source],
            dst_ref=valids.at[source],
            send_sem=valid_send.at[target],
            recv_sem=valid_recv.at[source],
            device_id={"chan": target},
            device_id_type=pl.DeviceIdType.MESH,
        )

    def spec_copy(source, target):
        return pltpu.make_async_remote_copy(
            src_ref=send.at[target],
            dst_ref=recv.at[source],
            send_sem=spec_send.at[target],
            recv_sem=spec_recv.at[source],
            device_id={"chan": target},
            device_id_type=pl.DeviceIdType.MESH,
        )

    def out_copy(source, target):
        at = pl.multiple_of(source * share, share)
        return pltpu.make_async_remote_copy(
            src_ref=stacked.at[target],
            dst_ref=out.at[:, pl.ds(at, share), :],
            send_sem=out_send.at[target],
            recv_sem=out_recv.at[source],
            device_id={"chan": target},
            device_id_type=pl.DeviceIdType.MESH,
        )

    lane = lax.broadcasted_iota(jnp.int32, (1, LANES), 1)
    first = lane < share
    channel = lax.broadcasted_iota(jnp.int32, (channels, 1), 0)
    lows = jnp.zeros((channels, 1), jnp.int32)
    highs = jnp.zeros((channels, 1), jnp.int32)
    for c in range(channels):
        lows = jnp.where(channel == c, low[c], lows)
        highs = jnp.where(channel == c, high[c], highs)

    def whitened(target):
        total = jnp.dot(mags[target], band[0], preferred_element_type=jnp.float32)
        total += jnp.dot(mags[target + 1], band[1], preferred_element_type=jnp.float32)
        total += jnp.dot(mags[target + 2], band[2], preferred_element_type=jnp.float32)
        k = target * share + jnp.where(first, lane, lane - share)
        near = jnp.minimum(k + SMOOTH, bin_total - 1) - jnp.maximum(k - SMOOTH, 0) + 1
        smoothed = total * (1.0 / near.astype(jnp.float32))
        inside = jnp.where((k >= lows) & (k < highs), 1.0, 0.0)
        y = spec[target] / jnp.maximum(smoothed, 1.0)
        y = y.reshape(windows, channels, LANES) * inside[None]
        return y.reshape(rows, LANES).astype(jnp.bfloat16)

    def send_valid(step, _):
        valid_copy(me, peer(step)).start()
        return 0

    lax.fori_loop(1, n, send_valid, 0)

    def send_spec(step, _):
        target = peer(step)
        send[target] = whitened(target)
        spec_copy(me, target).start()
        return 0

    lax.fori_loop(1, n, send_spec, 0)
    full[me] = whitened(me).astype(jnp.float32)

    def receive(step, _):
        source = peer(n - step)
        valid_copy(source, me).wait_recv()
        spec_copy(source, me).wait_recv()
        full[source] = recv[source].astype(jnp.float32)
        return 0

    lax.fori_loop(1, n, receive, 0)

    def stack_reader(reader):
        swapped = pltpu.roll(full[reader], share, 1)
        turned[...] = jnp.where(first, swapped, -swapped)
        flags = valids[reader]
        for pair in range(slots // 2):
            ids = [partners[reader, 2 * pair + half] for half in range(2)]

            def window_step(window, totals):
                at = pl.multiple_of(window * channels, channels)
                others = [full[q, pl.ds(at, channels), :] for q in ids]
                totals = list(totals)
                for i in range(channels):
                    straight = full[reader, pl.ds(at + i, 1), :]
                    crossed = turned[pl.ds(at + i, 1), :]
                    for half in range(2):
                        base = half * 2 * channels
                        totals[base + i] += straight * others[half]
                        totals[base + channels + i] += crossed * others[half]
                return tuple(totals)

            zero = jnp.zeros((channels, LANES), jnp.float32)
            totals = lax.fori_loop(
                0, windows, window_step, (zero,) * (4 * channels), unroll=4
            )
            weights = []
            for i in range(channels):
                both = []
                for half in range(2):
                    common = jnp.sum(flags[i : i + 1] * valids[ids[half]], axis=1, keepdims=True)
                    used = jnp.where(2 * pair + half < counts[reader], 1.0, 0.0)
                    both.append(used / jnp.maximum(common, 1.0))
                weights.append(jnp.where(first, both[0], both[1]))
            tiles = []
            for row in range(2 * channels):
                one, two = totals[row], totals[2 * channels + row]
                folded = jnp.where(first, one, two) + pltpu.roll(
                    jnp.where(first, two, one), share, 1
                )
                tiles.append(folded * weights[row % channels])
            flat = jnp.concatenate(tiles, axis=0).T.astype(jnp.bfloat16)
            stacked[reader, 2 * pair] = flat[:share]
            stacked[reader, 2 * pair + 1] = flat[share:]

    def send_stack(step, _):
        reader = peer(step)
        stack_reader(reader)
        out_copy(me, reader).start()
        return 0

    lax.fori_loop(1, n, send_stack, 0)
    stack_reader(me)
    own_at = pl.multiple_of(me * share, share)
    own = pltpu.make_async_copy(stacked.at[me], out.at[:, pl.ds(own_at, share), :], own_sem)
    own.start()
    own.wait()

    def finish_copies(step, _):
        target = peer(step)
        valid_copy(me, target).wait_send()
        spec_copy(me, target).wait_send()
        out_copy(me, target).wait_send()
        out_copy(target, me).wait_recv()
        return 0

    lax.fori_loop(1, n, finish_copies, 0)


def fused(n, records, window_valid, band_low, band_high, pair_counts, partners):
    channels, windows, length = records.shape
    bin_total = length // 2
    slots = partners.shape[1]
    share = bin_total // n
    rows = channels * windows
    table = jnp.asarray(packed_table(length, share, n))
    band = jnp.asarray(packed_band(share))
    vmem = pl.BlockSpec(memory_space=pltpu.VMEM)
    smem = pl.BlockSpec(memory_space=pltpu.SMEM)
    hbm = pl.BlockSpec(memory_space=pl.ANY)
    dma = pltpu.SemaphoreType.DMA
    out = pl.pallas_call(
        functools.partial(fused_kernel, n, bin_total),
        out_shape=jax.ShapeDtypeStruct((slots, bin_total, LANES), jnp.bfloat16),
        in_specs=[vmem, vmem, smem, smem, smem, smem, hbm, vmem],
        out_specs=hbm,
        scratch_shapes=[
            pltpu.VMEM(table.shape, jnp.bfloat16),
            pltpu.VMEM((rows, LANES), jnp.float32),
            pltpu.VMEM((rows, length), jnp.bfloat16),
            pltpu.VMEM((n, rows, LANES), jnp.float32),
            pltpu.VMEM((n + 2, rows, LANES), jnp.bfloat16),
            pltpu.VMEM((n, rows, LANES), jnp.bfloat16),
            pltpu.VMEM((n, rows, LANES), jnp.bfloat16),
            pltpu.VMEM((n, channels, windows), jnp.float32),
            pltpu.VMEM((n, rows, LANES), jnp.float32),
            pltpu.VMEM((rows, LANES), jnp.float32),
            pltpu.VMEM((n, slots, share, LANES), jnp.bfloat16),
            dma((n // 2,)),
            dma((n,)),
            dma((n,)),
            dma((n,)),
            dma((n,)),
            dma((n,)),
            dma((n,)),
            dma,
        ],
        compiler_params=pltpu.CompilerParams(
            collective_id=0, has_side_effects=True, vmem_limit_bytes=48 * 1024 * 1024
        ),
    )(records, window_valid, band_low, band_high, pair_counts, partners, table, band)
    return out[None]


def solution(mesh):
    def run(records, window_valid, band_low, band_high, pair_counts, partners):
        n = mesh.shape["chan"]
        channels, windows, length = records.shape
        whole_tiles = 2 * (length // 2 // n) == LANES and 2 * channels * channels == LANES
        args = (records, window_valid, band_low, band_high, pair_counts, partners)
        if whole_tiles and n % 2 == 0 and partners.shape[1] % 2 == 0:
            return fused(n, *args)
        return body(*args)

    return jax.shard_map(
        run,
        mesh=mesh,
        in_specs=(
            P(("groups", "chan"), None, None),
            P(("groups", "chan"), None),
            P(("groups", "chan")),
            P(("groups", "chan")),
            P("groups"),
            P("groups", None),
        ),
        out_specs=P(("groups", "chan"), None, None, None),
        check_vma=False,
    )
```

```python
import functools
import math

import jax
import jax.numpy as jnp
import ml_dtypes
import numpy as np
from jax import lax
from jax.experimental import pallas as pl
from jax.experimental.pallas import tpu as pltpu
from jax.sharding import PartitionSpec as P

SMOOTH = 8


def dft_table(length, first_bin, bin_count):
    sample_index = lax.broadcasted_iota(jnp.int32, (length, bin_count), 0)
    bin_index = lax.broadcasted_iota(jnp.int32, (length, bin_count), 1) + first_bin
    phase_step = sample_index * bin_index % length
    angles = phase_step.astype(jnp.float32) * (2.0 * math.pi / length)
    return jnp.concatenate([jnp.cos(angles), -jnp.sin(angles)], axis=1).astype(jnp.bfloat16)


def finish(spectrum, band_low, band_high, channels, windows):
    bin_total = spectrum.shape[1]
    magnitude = jnp.sqrt(spectrum[0] * spectrum[0] + spectrum[1] * spectrum[1])
    padded = jnp.pad(magnitude, ((SMOOTH, SMOOTH), (0, 0)))
    summed = padded[0:bin_total]
    for offset in range(1, 2 * SMOOTH + 1):
        summed = summed + padded[offset : offset + bin_total]
    bin_column = lax.broadcasted_iota(jnp.int32, (bin_total, 1), 0)
    in_range = (
        jnp.minimum(bin_column + SMOOTH, bin_total - 1) - jnp.maximum(bin_column - SMOOTH, 0) + 1
    )
    smoothed = summed / in_range.astype(jnp.float32)
    divisor = jnp.maximum(smoothed, 1.0).reshape(bin_total, channels, windows)
    bin_index = lax.broadcasted_iota(jnp.int32, (bin_total, channels, 1), 0)
    inside = (
        (bin_index >= band_low[None, :, None]) & (bin_index < band_high[None, :, None])
    ).astype(jnp.float32)
    shaped = spectrum.reshape(2, bin_total, channels, windows)
    return (
        (shaped / divisor * inside).astype(jnp.bfloat16).reshape(2, bin_total, channels * windows)
    )


def whiten(records, window_valid, band_low, band_high):
    channels, windows, length = records.shape
    bin_total = length // 2
    row_total = channels * windows
    one_bit = (jnp.sign(records.astype(jnp.float32)) * window_valid[:, :, None]).astype(
        jnp.bfloat16
    )
    one_bit = one_bit.reshape(row_total, length)
    blocks = []
    for first_bin in range(0, bin_total, 256):
        dft_block = dft_table(length, first_bin, 256)
        partial_spec = lax.dot_general(
            dft_block, one_bit, (((0,), (1,)), ((), ())), preferred_element_type=jnp.float32
        )
        blocks.append(partial_spec.reshape(2, 256, row_total))
    spectrum = jnp.concatenate(blocks, axis=1)
    return finish(spectrum, band_low, band_high, channels, windows)


def cross_stack(first_spec, second_spec, first_flags, second_flags, in_use):
    real_part = jnp.einsum(
        "fsim,fsjm->sfij", first_spec[0], second_spec[0], preferred_element_type=jnp.float32
    )
    real_part = real_part + jnp.einsum(
        "fsim,fsjm->sfij", first_spec[1], second_spec[1], preferred_element_type=jnp.float32
    )
    imag_part = jnp.einsum(
        "fsim,fsjm->sfij", first_spec[1], second_spec[0], preferred_element_type=jnp.float32
    )
    imag_part = imag_part - jnp.einsum(
        "fsim,fsjm->sfij", first_spec[0], second_spec[1], preferred_element_type=jnp.float32
    )
    common = jnp.einsum("sim,sjm->sij", first_flags, second_flags, precision=lax.Precision.HIGHEST)
    weight = in_use[:, None, None] / jnp.maximum(common, 1.0)
    both = jnp.stack([real_part, imag_part], axis=2) * weight[:, None, None]
    return both.reshape(both.shape[0], both.shape[1], -1).astype(jnp.bfloat16)


def body(records, window_valid, band_low, band_high, pair_counts, partners):
    channels, windows, length = records.shape
    bin_total = length // 2
    readers, slot_count = partners.shape
    bin_share = bin_total // readers
    whitened = whiten(records, window_valid, band_low, band_high)
    arrived = lax.all_to_all(whitened, "chan", split_axis=1, concat_axis=2, tiled=True)
    spectra = arrived.reshape(2, bin_share, readers, channels, windows)
    copies = jnp.broadcast_to(window_valid[None], (readers, channels, windows))
    valid_all = lax.all_to_all(copies, "chan", split_axis=0, concat_axis=0, tiled=True)
    results = []
    for slot_index in range(slot_count):
        partner_ids = partners[:, slot_index]
        picks = partner_ids[:, None] == jnp.arange(readers, dtype=jnp.int32)[None, :]
        partner_spec = jnp.einsum("rq,cfqim->cfrim", picks.astype(jnp.bfloat16), spectra)
        partner_flags = jnp.einsum(
            "rq,qim->rim", picks.astype(jnp.float32), valid_all, precision=lax.Precision.HIGHEST
        )
        in_use = (slot_index < pair_counts).astype(jnp.float32)
        results.append(cross_stack(spectra, partner_spec, valid_all, partner_flags, in_use))
    stacked = jnp.stack(results, axis=1)
    return lax.all_to_all(stacked, "chan", split_axis=0, concat_axis=2, tiled=True)


LANES = 128


def packed_table(length, share, readers):
    bins = np.arange(readers * share).reshape(readers // 2, 2, share)
    samples = np.arange(length)
    phase = (samples[None, :, None, None] * bins[:, None]) % length
    angles = phase.astype(np.float32) * np.float32(2.0 * math.pi / length)
    table = np.stack([np.cos(angles), -np.sin(angles)], axis=3)
    return table.reshape(readers // 2, length, 4 * share).astype(ml_dtypes.bfloat16)


def packed_band(share):
    lane = np.arange(2 * share) % share
    rows = np.arange(3)[:, None] * share - share + lane[None, :]
    near = np.abs(rows[:, :, None] - lane[None, None, :]) <= SMOOTH
    return (near * 0.5).astype(ml_dtypes.bfloat16)


def fused_kernel(
    n,
    bin_total,
    records_in,
    valid_in,
    low_in,
    high_in,
    counts_in,
    partners_in,
    table,
    band_in,
    out,
    records,
    valid,
    low,
    high,
    counts,
    partners,
    band,
    tables,
    raw,
    signs,
    spec,
    mags,
    send,
    recv,
    valids,
    full,
    turned,
    stacked,
    table_sem,
    valid_send,
    valid_recv,
    spec_send,
    spec_recv,
    out_send,
    out_recv,
    own_sem,
    in_sem,
):
    me = lax.axis_index("chan")
    channels, windows, length = records.shape
    share = bin_total // n
    rows = channels * windows
    slots = partners.shape[1]

    half_size = n // 2

    def peer(step, sign=1):
        near = (step - 1) % 2
        shift = (step - 1) // 2 + near
        side = (me // half_size + 1 + near) % 2
        return side * half_size + (me + half_size + sign * shift) % half_size

    barrier = pltpu.get_barrier_semaphore()
    for step in range(1, n):
        pl.semaphore_signal(
            barrier, inc=1, device_id={"chan": peer(step)}, device_id_type=pl.DeviceIdType.MESH
        )

    def table_copy(chunk):
        return pltpu.make_async_copy(table.at[chunk], tables.at[chunk], table_sem.at[chunk])

    inputs = [
        pltpu.make_async_copy(source, target, in_sem.at[i])
        for i, (source, target) in enumerate(
            [
                (records_in, records),
                (valid_in, valid),
                (low_in, low),
                (high_in, high),
                (counts_in, counts),
                (partners_in, partners),
                (band_in, band),
            ]
        )
    ]
    for copy in inputs:
        copy.start()
    for chunk in range(n // 2):
        table_copy(chunk).start()
    for copy in inputs:
        copy.wait()

    valids[me] = valid[...]

    def to_signs(part, _):
        at = pl.multiple_of(part * LANES, LANES)
        raw[...] = records[:, :, pl.ds(at, LANES)].astype(jnp.float32).reshape(rows, LANES)
        for pair in range(windows // 2):
            halves = []
            for window in (2 * pair, 2 * pair + 1):
                x = raw[pl.ds(window, channels, stride=windows), :]
                v = valid[:, window : window + 1]
                halves.append(jnp.where(x > 0, v, jnp.where(x < 0, -v, 0.0)))
            signs[pl.ds(pair * 2 * channels, 2 * channels), pl.ds(at, LANES)] = jnp.concatenate(
                halves, axis=0
            ).astype(jnp.bfloat16)
        return 0

    lax.fori_loop(0, length // LANES, to_signs, 0)

    mags[0] = jnp.zeros((rows, LANES), jnp.bfloat16)
    mags[n + 1] = jnp.zeros((rows, LANES), jnp.bfloat16)

    def transform(chunk, _):
        table_copy(chunk).wait()
        x = jnp.dot(signs[...], tables[chunk], preferred_element_type=jnp.float32)
        for half in range(2):
            y = x[:, half * LANES : (half + 1) * LANES]
            spec[2 * chunk + half] = y
            power = y * y
            mags[2 * chunk + half + 1] = jnp.sqrt(power + pltpu.roll(power, share, 1)).astype(
                jnp.bfloat16
            )
        return 0

    lax.fori_loop(0, n // 2, transform, 0)

    pl.semaphore_wait(barrier, n - 1)

    def valid_copy(source, target):
        return pltpu.make_async_remote_copy(
            src_ref=valids.at[source],
            dst_ref=valids.at[source],
            send_sem=valid_send.at[target],
            recv_sem=valid_recv.at[source],
            device_id={"chan": target},
            device_id_type=pl.DeviceIdType.MESH,
        )

    def spec_copy(source, target):
        return pltpu.make_async_remote_copy(
            src_ref=send.at[target],
            dst_ref=recv.at[source],
            send_sem=spec_send.at[target],
            recv_sem=spec_recv.at[source],
            device_id={"chan": target},
            device_id_type=pl.DeviceIdType.MESH,
        )

    def out_copy(source, target):
        at = pl.multiple_of(source * share, share)
        return pltpu.make_async_remote_copy(
            src_ref=stacked.at[target],
            dst_ref=out.at[:, pl.ds(at, share), :],
            send_sem=out_send.at[target],
            recv_sem=out_recv.at[source],
            device_id={"chan": target},
            device_id_type=pl.DeviceIdType.MESH,
        )

    lane = lax.broadcasted_iota(jnp.int32, (1, LANES), 1)
    first = lane < share
    channel = lax.broadcasted_iota(jnp.int32, (channels, 1), 0)
    lows = jnp.zeros((channels, 1), jnp.int32)
    highs = jnp.zeros((channels, 1), jnp.int32)
    for c in range(channels):
        lows = jnp.where(channel == c, low[c], lows)
        highs = jnp.where(channel == c, high[c], highs)

    def whitened(target):
        total = jnp.dot(mags[target], band[0], preferred_element_type=jnp.float32)
        total += jnp.dot(mags[target + 1], band[1], preferred_element_type=jnp.float32)
        total += jnp.dot(mags[target + 2], band[2], preferred_element_type=jnp.float32)
        k = target * share + jnp.where(first, lane, lane - share)
        near = jnp.minimum(k + SMOOTH, bin_total - 1) - jnp.maximum(k - SMOOTH, 0) + 1
        smoothed = total * (1.0 / near.astype(jnp.float32))
        inside = jnp.where((k >= lows) & (k < highs), 1.0, 0.0)
        y = spec[target] / jnp.maximum(smoothed, 1.0)
        y = y.reshape(windows, channels, LANES) * inside[None]
        return y.reshape(rows, LANES).astype(jnp.bfloat16)

    def send_valid(step, _):
        valid_copy(me, peer(step)).start()
        return 0

    lax.fori_loop(1, n, send_valid, 0)

    def send_spec(step, _):
        target = peer(step)
        send[target] = whitened(target)
        spec_copy(me, target).start()
        return 0

    lax.fori_loop(1, n, send_spec, 0)
    full[me] = whitened(me).astype(jnp.float32)

    def receive(step, _):
        source = peer(step, -1)
        valid_copy(source, me).wait_recv()
        spec_copy(source, me).wait_recv()
        full[source] = recv[source].astype(jnp.float32)
        return 0

    lax.fori_loop(1, n, receive, 0)

    def stack_reader(reader):
        swapped = pltpu.roll(full[reader], share, 1)
        turned[...] = jnp.where(first, swapped, -swapped)
        flags = valids[reader]
        for pair in range(slots // 2):
            ids = [partners[reader, 2 * pair + half] for half in range(2)]

            def window_step(window, totals):
                at = pl.multiple_of(window * channels, channels)
                others = [full[q, pl.ds(at, channels), :] for q in ids]
                totals = list(totals)
                for i in range(channels):
                    straight = full[reader, pl.ds(at + i, 1), :]
                    crossed = turned[pl.ds(at + i, 1), :]
                    for half in range(2):
                        base = half * 2 * channels
                        totals[base + i] += straight * others[half]
                        totals[base + channels + i] += crossed * others[half]
                return tuple(totals)

            zero = jnp.zeros((channels, LANES), jnp.float32)
            totals = lax.fori_loop(
                0, windows, window_step, (zero,) * (4 * channels), unroll=4
            )
            weights = []
            for i in range(channels):
                both = []
                for half in range(2):
                    common = jnp.sum(flags[i : i + 1] * valids[ids[half]], axis=1, keepdims=True)
                    used = jnp.where(2 * pair + half < counts[reader], 1.0, 0.0)
                    both.append(used / jnp.maximum(common, 1.0))
                weights.append(jnp.where(first, both[0], both[1]))
            tiles = []
            for row in range(2 * channels):
                one, two = totals[row], totals[2 * channels + row]
                folded = jnp.where(first, one, two) + pltpu.roll(
                    jnp.where(first, two, one), share, 1
                )
                tiles.append(folded * weights[row % channels])
            flat = jnp.concatenate(tiles, axis=0).T.astype(jnp.bfloat16)
            stacked[reader, 2 * pair] = flat[:share]
            stacked[reader, 2 * pair + 1] = flat[share:]

    def send_stack(step, _):
        reader = peer(step)
        stack_reader(reader)
        out_copy(me, reader).start()
        return 0

    lax.fori_loop(1, n, send_stack, 0)
    stack_reader(me)
    own_at = pl.multiple_of(me * share, share)
    own = pltpu.make_async_copy(stacked.at[me], out.at[:, pl.ds(own_at, share), :], own_sem)
    own.start()
    own.wait()

    def finish_copies(step, _):
        target = peer(step)
        valid_copy(me, target).wait_send()
        spec_copy(me, target).wait_send()
        out_copy(me, target).wait_send()
        out_copy(target, me).wait_recv()
        return 0

    lax.fori_loop(1, n, finish_copies, 0)


def fused(n, records, window_valid, band_low, band_high, pair_counts, partners):
    channels, windows, length = records.shape
    bin_total = length // 2
    slots = partners.shape[1]
    share = bin_total // n
    rows = channels * windows
    table = jnp.asarray(packed_table(length, share, n))
    band = jnp.asarray(packed_band(share))
    hbm = pl.BlockSpec(memory_space=pltpu.HBM)
    dma = pltpu.SemaphoreType.DMA
    out = pl.pallas_call(
        functools.partial(fused_kernel, n, bin_total),
        out_shape=jax.ShapeDtypeStruct((slots, bin_total, LANES), jnp.bfloat16),
        in_specs=[hbm] * 8,
        out_specs=pl.BlockSpec(memory_space=pl.ANY),
        scratch_shapes=[
            pltpu.VMEM(records.shape, jnp.bfloat16),
            pltpu.VMEM(window_valid.shape, jnp.float32),
            pltpu.SMEM(band_low.shape, jnp.int32),
            pltpu.SMEM(band_high.shape, jnp.int32),
            pltpu.SMEM(pair_counts.shape, jnp.int32),
            pltpu.SMEM(partners.shape, jnp.int32),
            pltpu.VMEM(band.shape, jnp.bfloat16),
            pltpu.VMEM(table.shape, jnp.bfloat16),
            pltpu.VMEM((rows, LANES), jnp.float32),
            pltpu.VMEM((rows, length), jnp.bfloat16),
            pltpu.VMEM((n, rows, LANES), jnp.float32),
            pltpu.VMEM((n + 2, rows, LANES), jnp.bfloat16),
            pltpu.VMEM((n, rows, LANES), jnp.bfloat16),
            pltpu.VMEM((n, rows, LANES), jnp.bfloat16),
            pltpu.VMEM((n, channels, windows), jnp.float32),
            pltpu.VMEM((n, rows, LANES), jnp.float32),
            pltpu.VMEM((rows, LANES), jnp.float32),
            pltpu.VMEM((n, slots, share, LANES), jnp.bfloat16),
            dma((n // 2,)),
            dma((n,)),
            dma((n,)),
            dma((n,)),
            dma((n,)),
            dma((n,)),
            dma((n,)),
            dma,
            dma((7,)),
        ],
        compiler_params=pltpu.CompilerParams(
            collective_id=0, has_side_effects=True, vmem_limit_bytes=64 * 1024 * 1024
        ),
    )(records, window_valid, band_low, band_high, pair_counts, partners, table, band)
    return out[None]


def solution(mesh):
    def run(records, window_valid, band_low, band_high, pair_counts, partners):
        n = mesh.shape["chan"]
        channels, windows, length = records.shape
        whole_tiles = 2 * (length // 2 // n) == LANES and 2 * channels * channels == LANES
        args = (records, window_valid, band_low, band_high, pair_counts, partners)
        if whole_tiles and n % 2 == 0 and partners.shape[1] % 2 == 0:
            return fused(n, *args)
        return body(*args)

    return jax.shard_map(
        run,
        mesh=mesh,
        in_specs=(
            P(("groups", "chan"), None, None),
            P(("groups", "chan"), None),
            P(("groups", "chan")),
            P(("groups", "chan")),
            P("groups"),
            P("groups", None),
        ),
        out_specs=P(("groups", "chan"), None, None, None),
        check_vma=False,
    )
```

```python
import functools
import math

import jax
import jax.numpy as jnp
import ml_dtypes
import numpy as np
from jax import lax
from jax.experimental import pallas as pl
from jax.experimental.pallas import tpu as pltpu
from jax.sharding import PartitionSpec as P

SMOOTH = 8


def dft_table(length, first_bin, bin_count):
    sample_index = lax.broadcasted_iota(jnp.int32, (length, bin_count), 0)
    bin_index = lax.broadcasted_iota(jnp.int32, (length, bin_count), 1) + first_bin
    phase_step = sample_index * bin_index % length
    angles = phase_step.astype(jnp.float32) * (2.0 * math.pi / length)
    return jnp.concatenate([jnp.cos(angles), -jnp.sin(angles)], axis=1).astype(jnp.bfloat16)


def finish(spectrum, band_low, band_high, channels, windows):
    bin_total = spectrum.shape[1]
    magnitude = jnp.sqrt(spectrum[0] * spectrum[0] + spectrum[1] * spectrum[1])
    padded = jnp.pad(magnitude, ((SMOOTH, SMOOTH), (0, 0)))
    summed = padded[0:bin_total]
    for offset in range(1, 2 * SMOOTH + 1):
        summed = summed + padded[offset : offset + bin_total]
    bin_column = lax.broadcasted_iota(jnp.int32, (bin_total, 1), 0)
    in_range = (
        jnp.minimum(bin_column + SMOOTH, bin_total - 1) - jnp.maximum(bin_column - SMOOTH, 0) + 1
    )
    smoothed = summed / in_range.astype(jnp.float32)
    divisor = jnp.maximum(smoothed, 1.0).reshape(bin_total, channels, windows)
    bin_index = lax.broadcasted_iota(jnp.int32, (bin_total, channels, 1), 0)
    inside = (
        (bin_index >= band_low[None, :, None]) & (bin_index < band_high[None, :, None])
    ).astype(jnp.float32)
    shaped = spectrum.reshape(2, bin_total, channels, windows)
    return (
        (shaped / divisor * inside).astype(jnp.bfloat16).reshape(2, bin_total, channels * windows)
    )


def whiten(records, window_valid, band_low, band_high):
    channels, windows, length = records.shape
    bin_total = length // 2
    row_total = channels * windows
    one_bit = (jnp.sign(records.astype(jnp.float32)) * window_valid[:, :, None]).astype(
        jnp.bfloat16
    )
    one_bit = one_bit.reshape(row_total, length)
    blocks = []
    for first_bin in range(0, bin_total, 256):
        dft_block = dft_table(length, first_bin, 256)
        partial_spec = lax.dot_general(
            dft_block, one_bit, (((0,), (1,)), ((), ())), preferred_element_type=jnp.float32
        )
        blocks.append(partial_spec.reshape(2, 256, row_total))
    spectrum = jnp.concatenate(blocks, axis=1)
    return finish(spectrum, band_low, band_high, channels, windows)


def cross_stack(first_spec, second_spec, first_flags, second_flags, in_use):
    real_part = jnp.einsum(
        "fsim,fsjm->sfij", first_spec[0], second_spec[0], preferred_element_type=jnp.float32
    )
    real_part = real_part + jnp.einsum(
        "fsim,fsjm->sfij", first_spec[1], second_spec[1], preferred_element_type=jnp.float32
    )
    imag_part = jnp.einsum(
        "fsim,fsjm->sfij", first_spec[1], second_spec[0], preferred_element_type=jnp.float32
    )
    imag_part = imag_part - jnp.einsum(
        "fsim,fsjm->sfij", first_spec[0], second_spec[1], preferred_element_type=jnp.float32
    )
    common = jnp.einsum("sim,sjm->sij", first_flags, second_flags, precision=lax.Precision.HIGHEST)
    weight = in_use[:, None, None] / jnp.maximum(common, 1.0)
    both = jnp.stack([real_part, imag_part], axis=2) * weight[:, None, None]
    return both.reshape(both.shape[0], both.shape[1], -1).astype(jnp.bfloat16)


def body(records, window_valid, band_low, band_high, pair_counts, partners):
    channels, windows, length = records.shape
    bin_total = length // 2
    readers, slot_count = partners.shape
    bin_share = bin_total // readers
    whitened = whiten(records, window_valid, band_low, band_high)
    arrived = lax.all_to_all(whitened, "chan", split_axis=1, concat_axis=2, tiled=True)
    spectra = arrived.reshape(2, bin_share, readers, channels, windows)
    copies = jnp.broadcast_to(window_valid[None], (readers, channels, windows))
    valid_all = lax.all_to_all(copies, "chan", split_axis=0, concat_axis=0, tiled=True)
    results = []
    for slot_index in range(slot_count):
        partner_ids = partners[:, slot_index]
        picks = partner_ids[:, None] == jnp.arange(readers, dtype=jnp.int32)[None, :]
        partner_spec = jnp.einsum("rq,cfqim->cfrim", picks.astype(jnp.bfloat16), spectra)
        partner_flags = jnp.einsum(
            "rq,qim->rim", picks.astype(jnp.float32), valid_all, precision=lax.Precision.HIGHEST
        )
        in_use = (slot_index < pair_counts).astype(jnp.float32)
        results.append(cross_stack(spectra, partner_spec, valid_all, partner_flags, in_use))
    stacked = jnp.stack(results, axis=1)
    return lax.all_to_all(stacked, "chan", split_axis=0, concat_axis=2, tiled=True)


LANES = 128


def packed_table(length, share, readers):
    bins = np.arange(readers * share).reshape(readers // 2, 2, share)
    samples = np.arange(length)
    phase = (samples[None, :, None, None] * bins[:, None]) % length
    angles = phase.astype(np.float32) * np.float32(2.0 * math.pi / length)
    table = np.stack([np.cos(angles), -np.sin(angles)], axis=3)
    return table.reshape(readers // 2, length, 4 * share).astype(ml_dtypes.bfloat16)


def packed_band(share):
    lane = np.arange(2 * share) % share
    rows = np.arange(3)[:, None] * share - share + lane[None, :]
    near = np.abs(rows[:, :, None] - lane[None, None, :]) <= SMOOTH
    return (near * 0.5).astype(ml_dtypes.bfloat16)


def fused_kernel(
    n,
    bin_total,
    records_in,
    valid_in,
    low_in,
    high_in,
    counts_in,
    partners_in,
    table,
    band_in,
    out,
    records,
    valid,
    low,
    high,
    counts,
    partners,
    band,
    tables,
    raw,
    signs,
    spec,
    mags,
    send,
    recv,
    valids,
    full,
    turned,
    stacked,
    table_sem,
    valid_send,
    valid_recv,
    spec_send,
    spec_recv,
    out_send,
    out_recv,
    own_sem,
    in_sem,
):
    me = lax.axis_index("chan")
    channels, windows, length = records.shape
    share = bin_total // n
    rows = channels * windows
    slots = partners.shape[1]

    half_size = n // 2

    def peer(step, sign=1):
        near = (step - 1) % 2
        shift = (step - 1) // 2 + near
        side = (me // half_size + 1 + near) % 2
        return side * half_size + (me + half_size + sign * shift) % half_size

    barrier = pltpu.get_barrier_semaphore()
    for step in range(1, n):
        pl.semaphore_signal(
            barrier, inc=1, device_id={"chan": peer(step)}, device_id_type=pl.DeviceIdType.MESH
        )

    def table_copy(chunk):
        return pltpu.make_async_copy(table.at[chunk], tables.at[chunk], table_sem.at[chunk])

    inputs = [
        pltpu.make_async_copy(source, target, in_sem.at[i])
        for i, (source, target) in enumerate(
            [
                (records_in, records),
                (valid_in, valid),
                (low_in, low),
                (high_in, high),
                (counts_in, counts),
                (partners_in, partners),
                (band_in, band),
            ]
        )
    ]
    for copy in inputs:
        copy.start()
    for chunk in range(n // 2):
        table_copy(chunk).start()
    for copy in inputs:
        copy.wait()

    valids[me] = valid[...]

    def to_signs(part, _):
        at = pl.multiple_of(part * LANES, LANES)
        raw[...] = records[:, :, pl.ds(at, LANES)].astype(jnp.float32).reshape(rows, LANES)
        for pair in range(windows // 2):
            halves = []
            for window in (2 * pair, 2 * pair + 1):
                x = raw[pl.ds(window, channels, stride=windows), :]
                v = valid[:, window : window + 1]
                halves.append(jnp.where(x > 0, v, jnp.where(x < 0, -v, 0.0)))
            signs[pl.ds(pair * 2 * channels, 2 * channels), pl.ds(at, LANES)] = jnp.concatenate(
                halves, axis=0
            ).astype(jnp.bfloat16)
        return 0

    lax.fori_loop(0, length // LANES, to_signs, 0, unroll=2)

    mags[0] = jnp.zeros((rows, LANES), jnp.bfloat16)
    mags[n + 1] = jnp.zeros((rows, LANES), jnp.bfloat16)

    def transform(chunk, _):
        table_copy(chunk).wait()
        x = jnp.dot(signs[...], tables[chunk], preferred_element_type=jnp.float32)
        for half in range(2):
            y = x[:, half * LANES : (half + 1) * LANES]
            spec[2 * chunk + half] = y
            power = y * y
            mags[2 * chunk + half + 1] = jnp.sqrt(power + pltpu.roll(power, share, 1)).astype(
                jnp.bfloat16
            )
        return 0

    lax.fori_loop(0, n // 2, transform, 0, unroll=2)

    pl.semaphore_wait(barrier, n - 1)

    def valid_copy(source, target):
        return pltpu.make_async_remote_copy(
            src_ref=valids.at[source],
            dst_ref=valids.at[source],
            send_sem=valid_send.at[target],
            recv_sem=valid_recv.at[source],
            device_id={"chan": target},
            device_id_type=pl.DeviceIdType.MESH,
        )

    def spec_copy(source, target):
        return pltpu.make_async_remote_copy(
            src_ref=send.at[target],
            dst_ref=recv.at[source],
            send_sem=spec_send.at[target],
            recv_sem=spec_recv.at[source],
            device_id={"chan": target},
            device_id_type=pl.DeviceIdType.MESH,
        )

    def out_copy(source, target):
        at = pl.multiple_of(source * share, share)
        return pltpu.make_async_remote_copy(
            src_ref=stacked.at[target],
            dst_ref=out.at[:, pl.ds(at, share), :],
            send_sem=out_send.at[target],
            recv_sem=out_recv.at[source],
            device_id={"chan": target},
            device_id_type=pl.DeviceIdType.MESH,
        )

    lane = lax.broadcasted_iota(jnp.int32, (1, LANES), 1)
    first = lane < share
    channel = lax.broadcasted_iota(jnp.int32, (channels, 1), 0)
    lows = jnp.zeros((channels, 1), jnp.int32)
    highs = jnp.zeros((channels, 1), jnp.int32)
    for c in range(channels):
        lows = jnp.where(channel == c, low[c], lows)
        highs = jnp.where(channel == c, high[c], highs)

    def whitened(target):
        total = jnp.dot(mags[target], band[0], preferred_element_type=jnp.float32)
        total += jnp.dot(mags[target + 1], band[1], preferred_element_type=jnp.float32)
        total += jnp.dot(mags[target + 2], band[2], preferred_element_type=jnp.float32)
        k = target * share + jnp.where(first, lane, lane - share)
        near = jnp.minimum(k + SMOOTH, bin_total - 1) - jnp.maximum(k - SMOOTH, 0) + 1
        smoothed = total * (1.0 / near.astype(jnp.float32))
        inside = jnp.where((k >= lows) & (k < highs), 1.0, 0.0)
        y = spec[target] / jnp.maximum(smoothed, 1.0)
        y = y.reshape(windows, channels, LANES) * inside[None]
        return y.reshape(rows, LANES).astype(jnp.bfloat16)

    def send_valid(step, _):
        valid_copy(me, peer(step)).start()
        return 0

    lax.fori_loop(1, n, send_valid, 0)

    def send_spec(step, _):
        target = peer(step)
        send[target] = whitened(target)
        spec_copy(me, target).start()
        return 0

    lax.fori_loop(1, n, send_spec, 0)
    full[me] = whitened(me).astype(jnp.float32)

    def receive(step, _):
        source = peer(step, -1)
        valid_copy(source, me).wait_recv()
        spec_copy(source, me).wait_recv()
        full[source] = recv[source].astype(jnp.float32)
        return 0

    lax.fori_loop(1, n, receive, 0)

    def stack_reader(reader):
        swapped = pltpu.roll(full[reader], share, 1)
        turned[...] = jnp.where(first, swapped, -swapped)
        flags = valids[reader]
        for pair in range(slots // 2):
            ids = [partners[reader, 2 * pair + half] for half in range(2)]

            def window_step(window, totals):
                at = pl.multiple_of(window * channels, channels)
                others = [full[q, pl.ds(at, channels), :] for q in ids]
                totals = list(totals)
                for i in range(channels):
                    straight = full[reader, pl.ds(at + i, 1), :]
                    crossed = turned[pl.ds(at + i, 1), :]
                    for half in range(2):
                        base = half * 2 * channels
                        totals[base + i] += straight * others[half]
                        totals[base + channels + i] += crossed * others[half]
                return tuple(totals)

            zero = jnp.zeros((channels, LANES), jnp.float32)
            totals = lax.fori_loop(
                0, windows, window_step, (zero,) * (4 * channels), unroll=8
            )
            weights = []
            for i in range(channels):
                both = []
                for half in range(2):
                    common = jnp.sum(flags[i : i + 1] * valids[ids[half]], axis=1, keepdims=True)
                    used = jnp.where(2 * pair + half < counts[reader], 1.0, 0.0)
                    both.append(used / jnp.maximum(common, 1.0))
                weights.append(jnp.where(first, both[0], both[1]))
            tiles = []
            for row in range(2 * channels):
                one, two = totals[row], totals[2 * channels + row]
                folded = jnp.where(first, one, two) + pltpu.roll(
                    jnp.where(first, two, one), share, 1
                )
                tiles.append(folded * weights[row % channels])
            flat = jnp.concatenate(tiles, axis=0).T.astype(jnp.bfloat16)
            stacked[reader, 2 * pair] = flat[:share]
            stacked[reader, 2 * pair + 1] = flat[share:]

    def send_stack(step, _):
        reader = peer(step)
        stack_reader(reader)
        out_copy(me, reader).start()
        return 0

    lax.fori_loop(1, n, send_stack, 0)
    stack_reader(me)
    own_at = pl.multiple_of(me * share, share)
    own = pltpu.make_async_copy(stacked.at[me], out.at[:, pl.ds(own_at, share), :], own_sem)
    own.start()
    own.wait()

    def finish_copies(step, _):
        target = peer(step)
        valid_copy(me, target).wait_send()
        spec_copy(me, target).wait_send()
        out_copy(me, target).wait_send()
        out_copy(target, me).wait_recv()
        return 0

    lax.fori_loop(1, n, finish_copies, 0)


def fused(n, records, window_valid, band_low, band_high, pair_counts, partners):
    channels, windows, length = records.shape
    bin_total = length // 2
    slots = partners.shape[1]
    share = bin_total // n
    rows = channels * windows
    table = jnp.asarray(packed_table(length, share, n))
    band = jnp.asarray(packed_band(share))
    hbm = pl.BlockSpec(memory_space=pltpu.HBM)
    dma = pltpu.SemaphoreType.DMA
    out = pl.pallas_call(
        functools.partial(fused_kernel, n, bin_total),
        out_shape=jax.ShapeDtypeStruct((slots, bin_total, LANES), jnp.bfloat16),
        in_specs=[hbm] * 8,
        out_specs=pl.BlockSpec(memory_space=pl.ANY),
        scratch_shapes=[
            pltpu.VMEM(records.shape, jnp.bfloat16),
            pltpu.VMEM(window_valid.shape, jnp.float32),
            pltpu.SMEM(band_low.shape, jnp.int32),
            pltpu.SMEM(band_high.shape, jnp.int32),
            pltpu.SMEM(pair_counts.shape, jnp.int32),
            pltpu.SMEM(partners.shape, jnp.int32),
            pltpu.VMEM(band.shape, jnp.bfloat16),
            pltpu.VMEM(table.shape, jnp.bfloat16),
            pltpu.VMEM((rows, LANES), jnp.float32),
            pltpu.VMEM((rows, length), jnp.bfloat16),
            pltpu.VMEM((n, rows, LANES), jnp.float32),
            pltpu.VMEM((n + 2, rows, LANES), jnp.bfloat16),
            pltpu.VMEM((n, rows, LANES), jnp.bfloat16),
            pltpu.VMEM((n, rows, LANES), jnp.bfloat16),
            pltpu.VMEM((n, channels, windows), jnp.float32),
            pltpu.VMEM((n, rows, LANES), jnp.float32),
            pltpu.VMEM((rows, LANES), jnp.float32),
            pltpu.VMEM((n, slots, share, LANES), jnp.bfloat16),
            dma((n // 2,)),
            dma((n,)),
            dma((n,)),
            dma((n,)),
            dma((n,)),
            dma((n,)),
            dma((n,)),
            dma,
            dma((7,)),
        ],
        compiler_params=pltpu.CompilerParams(
            collective_id=0, has_side_effects=True, vmem_limit_bytes=64 * 1024 * 1024
        ),
    )(records, window_valid, band_low, band_high, pair_counts, partners, table, band)
    return out[None]


def solution(mesh):
    def run(records, window_valid, band_low, band_high, pair_counts, partners):
        n = mesh.shape["chan"]
        channels, windows, length = records.shape
        whole_tiles = 2 * (length // 2 // n) == LANES and 2 * channels * channels == LANES
        args = (records, window_valid, band_low, band_high, pair_counts, partners)
        if whole_tiles and n % 2 == 0 and partners.shape[1] % 2 == 0:
            return fused(n, *args)
        return body(*args)

    return jax.shard_map(
        run,
        mesh=mesh,
        in_specs=(
            P(("groups", "chan"), None, None),
            P(("groups", "chan"), None),
            P(("groups", "chan")),
            P(("groups", "chan")),
            P("groups"),
            P("groups", None),
        ),
        out_specs=P(("groups", "chan"), None, None, None),
        check_vma=False,
    )
```
